512 devices in a mesh: ctx: 64 (over y, x, core), tp: 8 (over z).
Axes of the slice: x: 4, y: 8, z: 8, core: 2. Of those that a mesh axis runs over, the one named last changes fastest.
Arguments:
- queries: bfloat16 [32768, 4096], P('ctx', 'tp'), may hold values from -8 to 8
- keys: bfloat16 [32768, 4096], P('ctx', 'tp'), may hold values from -6 to 6
- values: bfloat16 [32768, 4096], P('ctx', 'tp'), may hold values from -6 to 6
- log_decay: float32 [32768, 32], P('ctx', 'tp'), may hold values from -4 to 0
- gain: float32 [4096], P('tp'), may hold values from 0.1 to 1.9
- upstream: bfloat16 [32768, 4096], P('ctx', 'tp'), may hold values from -40 to 40
Outputs:
- attn_out: bfloat16 [32768, 4096], P('ctx', 'tp')
- grad_queries: bfloat16 [32768, 4096], P('ctx', 'tp')
- grad_keys: bfloat16 [32768, 4096], P('ctx', 'tp')
- grad_values: bfloat16 [32768, 4096], P('ctx', 'tp')
- grad_gain: float32 [4096], P('tp')
The draws below stay inside these ranges and needn't reach their ends.
All inputs are finite; a program needn't handle non-finite values.
Results may differ from the reference program's by a relative error of at most 0.0051.
Values sent between devices are 32-bit elements; how exact they have to be, the bound alone decides.
A program may use at most 128 MiB of HBM per device.

```python
import math
import jax
import jax.numpy as jnp
from jax import lax

HEAD_COUNT = 32
DH = 128
BLK = 512
SEQUENCE_LENGTH = 32768
FEAT = 4096


def draw_queries(key, part):
    key = jax.random.fold_in(key, 11)
    key_a = jax.random.fold_in(key, 0)
    head_of = (jnp.arange(FEAT) // DH).astype(jnp.float32)
    column_scale = DH ** (-0.5) * jnp.exp(math.log(3.0) * head_of / (HEAD_COUNT - 1))
    base_draw = jnp.clip(jax.random.normal(key_a, (SEQUENCE_LENGTH, FEAT), jnp.float32), -6.0, 6.0)
    return (base_draw * column_scale[None, :]).astype(jnp.bfloat16)


def draw_upstream(key, part):
    key = jax.random.fold_in(key, 12)
    key_a = jax.random.fold_in(key, 0)
    rising = jnp.exp(math.log(3.0) * jnp.arange(SEQUENCE_LENGTH).astype(jnp.float32) / SEQUENCE_LENGTH)[:, None]
    base_draw = jnp.clip(jax.random.normal(key_a, (SEQUENCE_LENGTH, FEAT), jnp.float32), -6.0, 6.0)
    return (base_draw * rising).astype(jnp.bfloat16)


def draw_log_decay(key, part):
    key = jax.random.fold_in(key, 13)
    key_a, key_b, key_c, key_random_fourth, key_e = jax.random.split(key, 5)
    fast_share = 0.5
    is_fast = jax.random.uniform(key_a, (HEAD_COUNT,), jnp.float32) < fast_share
    baseline_rate = jnp.where(is_fast, -10.0 / BLK, -0.5 / SEQUENCE_LENGTH)
    segment = jnp.arange(SEQUENCE_LENGTH) // 256
    table = jnp.exp(jax.random.uniform(key_b, (SEQUENCE_LENGTH // 256 + 1,), jnp.float32, -math.log(2.0), math.log(2.0)))
    segment_multiplier = jnp.take(table, segment)[:, None]
    coarse_estimate = jnp.exp(jax.random.uniform(key_c, (SEQUENCE_LENGTH, HEAD_COUNT), jnp.float32, -math.log(2.0), math.log(2.0)))
    spike_amount = jax.random.uniform(key_random_fourth, (SEQUENCE_LENGTH, HEAD_COUNT), jnp.float32) < 4.0 / SEQUENCE_LENGTH
    layer_depth = jnp.log(jax.random.uniform(key_e, (SEQUENCE_LENGTH, HEAD_COUNT), jnp.float32, 0.5, 0.8))
    return baseline_rate[None, :] * segment_multiplier * coarse_estimate + jnp.where(spike_amount, layer_depth, 0.0)


def level_of(rng, dims, shards, smallest, high):
    level = 1.0
    for position, blocks in shards:
        draws = jax.random.uniform(jax.random.fold_in(jax.random.fold_in(rng, 6), position), (blocks,), jnp.float32, smallest / len(shards), high / len(shards))
        level = level * jnp.repeat(jnp.exp(draws), dims[position] // blocks).reshape((-1,) + (1,) * (len(dims) - 1 - position))
    return level


def bell_draw(key, extent, scale, bound, cuts=(), kind=jnp.bfloat16):
    array = scale * jax.random.normal(key, extent, jnp.float32)
    if cuts:
        array = array * level_of(key, extent, cuts, -0.22, 0.18)
    return jnp.clip(array, -bound, bound).astype(kind)


def setup_inputs(seed: int = 0) -> dict:
    seeds = jax.random.split(jax.random.key(seed), 7)
    queries = draw_queries(jax.random.fold_in(seeds[6], 71), 0)
    keys = bell_draw(seeds[1], (SEQUENCE_LENGTH, FEAT), 1.0, 6.0, ((0, 64), (1, 8)))
    values = bell_draw(seeds[2], (SEQUENCE_LENGTH, FEAT), 1.0, 6.0, ((0, 64), (1, 8)))
    log_decay = draw_log_decay(jax.random.fold_in(seeds[6], 71), 0)
    gain = jnp.clip(1.0 + 0.18 * jax.random.normal(seeds[4], (FEAT,), jnp.float32), 0.1, 1.9)
    upstream = draw_upstream(jax.random.fold_in(seeds[6], 71), 0)
    return dict(queries=queries, keys=keys, values=values, log_decay=log_decay, gain=gain, upstream=upstream)


def block_weights(lam_block, lower_mask):
    cum_log = jnp.cumsum(lam_block, axis=0)
    trans = cum_log.T
    diff = trans[:, :, None] - trans[:, None, :]
    return (cum_log, jnp.exp(jnp.where(lower_mask[None], diff, -jnp.inf)))

def reference(queries, keys, values, log_decay, gain, upstream):
    highest = lax.Precision.HIGHEST
    f32 = jnp.float32
    count = SEQUENCE_LENGTH // BLK
    query_blk = queries.reshape(count, BLK, HEAD_COUNT, DH)
    key_blk = keys.reshape(count, BLK, HEAD_COUNT, DH)
    value_blk = values.reshape(count, BLK, HEAD_COUNT, DH)
    lam_blk = log_decay.reshape(count, BLK, HEAD_COUNT)
    offsets = jnp.arange(BLK)
    lower_mask = offsets[:, None] >= offsets[None, :]

    def forward(run_state, pieces):
        qq, kk, vv, lam = pieces
        cum_log, weight_mat = block_weights(lam, lower_mask)
        last = cum_log[-1]
        raw_scores = jnp.einsum('ihd,jhd->hij', qq.astype(f32), kk.astype(f32))
        scores = (raw_scores * weight_mat).astype(jnp.bfloat16)
        inside = jnp.einsum('hij,jhd->ihd', scores.astype(f32), vv.astype(f32))
        outer = jnp.exp(cum_log)[:, :, None] * jnp.einsum('ihd,hde->ihe', qq.astype(f32), run_state, precision=highest)
        keyed_rows = kk.astype(f32) * jnp.exp(last[None, :] - cum_log)[:, :, None]
        local_state = jnp.einsum('jhd,jhe->hde', keyed_rows, vv.astype(f32), precision=highest)
        new_state = jnp.exp(last)[:, None, None] * run_state + local_state
        return (new_state, (inside + outer, run_state))
    start_state = jnp.zeros((HEAD_COUNT, DH, DH), f32)
    _, (acts, entering) = lax.scan(forward, start_state, (query_blk, key_blk, value_blk, lam_blk))
    attended = acts.reshape(SEQUENCE_LENGTH, FEAT)
    gain_row = gain[None, :]
    up_grad = upstream.astype(f32)
    scaled = gain_row * up_grad
    inv_rms = lax.rsqrt(lax.optimization_barrier(jnp.sum(attended * attended, axis=1, keepdims=True)) / FEAT + 1e-06)
    normed = attended * inv_rms
    attn_out = (normed * gain_row).astype(jnp.bfloat16)
    grad_gain = lax.optimization_barrier(jnp.sum(normed * up_grad, axis=0))
    cross_mean = lax.optimization_barrier(jnp.sum(attended * scaled, axis=1, keepdims=True)) / FEAT
    grad_attn = (inv_rms * scaled - attended * (inv_rms * inv_rms * inv_rms) * cross_mean).astype(jnp.bfloat16)
    grad_blk = grad_attn.reshape(count, BLK, HEAD_COUNT, DH)

    def backward(grad_end, pieces):
        qq, kk, vv, lam, run_state, dd = pieces
        cum_log, weight_mat = block_weights(lam, lower_mask)
        last = cum_log[-1]
        qf, kf, vf, df = (qq.astype(f32), kk.astype(f32), vv.astype(f32), dd.astype(f32))
        raw_scores = jnp.einsum('ihd,jhd->hij', qf, kf)
        scores = (raw_scores * weight_mat).astype(jnp.bfloat16)
        raw_grad = jnp.einsum('ihe,jhe->hij', df, vf)
        grad_mat = (raw_grad * weight_mat).astype(jnp.bfloat16).astype(f32)
        rise = jnp.exp(cum_log)[:, :, None]
        fall = jnp.exp(last[None, :] - cum_log)[:, :, None]
        grad_q = jnp.einsum('hij,jhd->ihd', grad_mat, kf) + rise * jnp.einsum('ihe,hde->ihd', df, run_state, precision=highest)
        grad_k = jnp.einsum('hij,ihd->jhd', grad_mat, qf) + fall * jnp.einsum('jhe,hde->jhd', vf, grad_end, precision=highest)
        grad_v = jnp.einsum('hij,ihe->jhe', scores.astype(f32), df) + fall * jnp.einsum('jhd,hde->jhe', kf, grad_end, precision=highest)
        moment = jnp.einsum('ihd,ihe->hde', qf * rise, df, precision=highest)
        previous = jnp.exp(last)[:, None, None] * grad_end + moment
        return (previous, (grad_q, grad_k, grad_v))
    _, (grad_q, grad_k, grad_v) = lax.scan(backward, start_state, (query_blk, key_blk, value_blk, lam_blk, entering, grad_blk), reverse=True)
    grad_queries = grad_q.reshape(SEQUENCE_LENGTH, FEAT).astype(jnp.bfloat16)
    grad_keys = grad_k.reshape(SEQUENCE_LENGTH, FEAT).astype(jnp.bfloat16)
    grad_values = grad_v.reshape(SEQUENCE_LENGTH, FEAT).astype(jnp.bfloat16)
    return (attn_out, grad_queries, grad_keys, grad_values, grad_gain)
```

```python
import functools

import jax
import jax.numpy as jnp
from jax import lax
from jax.experimental import pallas as pl
from jax.experimental.pallas import tpu as pltpu
from jax.sharding import PartitionSpec as P

MESH = pl.DeviceIdType.MESH
FEAT = 4096
BLK = 512
DH = 128
HEADS = 4
ROWB = 128
NRB = BLK // ROWB
CHIPS = 8
GROUPS = 4
TP = 8
SLICE = 2 * DH // CHIPS
F32 = jnp.float32
BF16 = jnp.bfloat16


def mm(a, b, ca, cb):
    return lax.dot_general(a, b, (((ca,), (cb,)), ((), ())), preferred_element_type=F32)


def split(x):
    hi = x.astype(BF16)
    return hi, (x - hi.astype(F32)).astype(BF16)


def bcast_col(row):
    return jnp.broadcast_to(row, (ROWB, row.shape[1])).T


class Scan:
    def __init__(self, refs, place):
        (
            self.out0, self.in0, self.out1, self.in1, self.out2, self.in2, self.out3, self.in3, self.out4, self.in4,
            self.s0, self.r0, self.s1, self.r1, self.s2, self.r2, self.s3, self.r3, self.s4, self.r4,
        ) = refs
        self.core, self.p, self.g, self.tp = place

    def device(self, g, p, core):
        return ((g * CHIPS + p) * 2 + core, self.tp)

    def core_copy(self, src, dst, send, recv):
        return pltpu.make_async_remote_copy(
            src_ref=src, dst_ref=dst, send_sem=send.at[0], recv_sem=recv.at[0],
            device_id=self.device(self.g, self.p, 1 - self.core), device_id_type=MESH,
        )

    def copy0(self):
        return self.core_copy(self.out0, self.in0, self.s0, self.r0)

    def copy4(self):
        return self.core_copy(self.out4, self.in4, self.s4, self.r4)

    def group_copy(self, d, src, dst, send, recv, arriving):
        peer = (self.p + d) % CHIPS
        slot = peer if arriving else self.p
        return pltpu.make_async_remote_copy(
            src_ref=src.at[peer], dst_ref=dst.at[slot], send_sem=send.at[d], recv_sem=recv.at[slot],
            device_id=self.device(self.g, peer, self.core), device_id_type=MESH,
        )

    def copy1(self, d, arriving=False):
        return self.group_copy(d, self.out1, self.in1, self.s1, self.r1, arriving)

    def copy3(self, d, arriving=False):
        return self.group_copy(d, self.out3, self.in3, self.s3, self.r3, arriving)

    def copy2(self, d, arriving=False):
        peer = (self.g + d) % GROUPS
        slot = peer if arriving else self.g
        return pltpu.make_async_remote_copy(
            src_ref=self.out2, dst_ref=self.in2.at[slot], send_sem=self.s2.at[d], recv_sem=self.r2.at[slot],
            device_id=self.device(peer, self.p, self.core), device_id_type=MESH,
        )


GROUP_ORDER = (6, 2, 4, 5, 3, 7, 1)
RING_ORDER = (2, 1, 3)
TP_ORDER = (4, 3, 5, 2, 6, 1, 7)


def kernel(*refs):
    (q_ref, k_ref, v_ref, log_ref, gain_ref, u_ref, out_ref, gq_ref, gk_ref, gv_ref, gg_ref) = refs[:11]
    (
        crow, rise, fall, dec, w_st, p_st, g_st, a_st, su_st, da_st, gk_st, gv_st, own_st, s_st, r_st, ggp,
        zout, zin, zs, zr,
    ) = refs[11:31]
    ctx = lax.axis_index("ctx")
    tp = lax.axis_index("tp")
    core = ctx % 2
    chip = ctx // 2
    p = chip % CHIPS
    g = chip // CHIPS
    place = (core, p, g, tp)
    fwd = Scan(refs[31:51], place)
    bwd = Scan(refs[51:71], place)
    first = core == 0

    def tp_copy(d, arriving=False):
        peer = (tp + d) % TP
        slot = peer if arriving else tp
        return pltpu.make_async_remote_copy(
            src_ref=zout, dst_ref=zin.at[slot], send_sem=zs.at[d], recv_sem=zr.at[slot],
            device_id=(ctx, peer), device_id_type=MESH,
        )

    barrier = pltpu.get_barrier_semaphore()
    partners = [fwd.device(g, p, 1 - core)]
    partners += [fwd.device(g, (p + d) % CHIPS, core) for d in range(1, CHIPS)]
    partners += [fwd.device((g + d) % GROUPS, p, core) for d in range(1, GROUPS)]
    partners += [(ctx, (tp + d) % TP) for d in range(1, TP)]
    for partner in partners:
        pl.semaphore_signal(barrier, inc=1, device_id=partner, device_id_type=MESH)

    cum = log_ref[...]
    lane = lax.broadcasted_iota(jnp.int32, cum.shape, 1)
    step = 1
    while step < BLK:
        cum = cum + jnp.where(lane >= step, pltpu.roll(cum, step, axis=1), 0.0)
        step *= 2
    for h in range(HEADS):
        row = cum[h : h + 1, :]
        crow[h] = row
        last = jnp.broadcast_to(row[:, BLK - 1 : BLK], (1, DH))
        dec[h] = jnp.exp(last)
        for rb in range(NRB):
            rows = slice(rb * ROWB, (rb + 1) * ROWB)
            col = bcast_col(row[:, rows])
            rise[h, rows, :] = col
            fall[h, rows, :] = jnp.exp(last - col)

    def lanes(h):
        if isinstance(h, int):
            return slice(h * DH, (h + 1) * DH)
        return pl.ds(pl.multiple_of(h * DH, DH), DH)

    def keyed_state(h):
        total = None
        for rb in range(NRB):
            rows = slice(rb * ROWB, (rb + 1) * ROWB)
            hi, lo = split(k_ref[rows, lanes(h)].astype(F32) * fall[h, rows, :])
            vv = v_ref[rows, lanes(h)]
            term = mm(hi, vv, 0, 0) + mm(lo, vv, 0, 0)
            total = term if total is None else total + term
        return total

    def moment(h):
        total = None
        for rb in range(NRB):
            rows = slice(rb * ROWB, (rb + 1) * ROWB)
            hi, lo = split(q_ref[rows, lanes(h)].astype(F32) * jnp.exp(rise[h, rows, :]))
            dd = da_st[rows, lanes(h)]
            term = mm(hi, dd, 0, 0) + mm(lo, dd, 0, 0)
            total = term if total is None else total + term
        return total

    mine = 2 * core
    other = 2 * (1 - core)
    for j in range(2):
        fwd.out0[j * DH : (j + 1) * DH, :] = keyed_state(other + j)
        fwd.out0[2 * DH + j : 2 * DH + j + 1, :] = dec[other + j]
    fwd.out0[2 * DH + 2 : 2 * DH + 8, :] = jnp.zeros((6, DH), F32)
    pl.semaphore_wait(barrier, len(partners))
    fwd.copy0().start()
    for j in range(2):
        own_st[j] = keyed_state(mine + j)

    def send_chip(scan, backward):
        scan.copy0().wait()
        for j in range(2):
            theirs = scan.in0[j * DH : (j + 1) * DH, :]
            ours = own_st[j]
            d_ours, d_theirs = dec[mine + j], fwd.in0[2 * DH + j : 2 * DH + j + 1, :]
            if backward:
                chip_state = jnp.where(first, d_ours * theirs + ours, d_theirs * ours + theirs)
                tail = scan.in0[2 * DH : 2 * DH + 8, :] + scan.out0[2 * DH : 2 * DH + 8, :]
            else:
                chip_state = jnp.where(first, d_theirs * ours + theirs, d_ours * theirs + ours)
                tail = jnp.broadcast_to(d_ours * d_theirs, (8, DH))
            for piece in range(CHIPS // 2):
                slot = j * (CHIPS // 2) + piece
                scan.out1[slot, 0:SLICE, :] = chip_state[piece * SLICE : (piece + 1) * SLICE, :]
                scan.out1[slot, SLICE : SLICE + 8, :] = tail
        for d in GROUP_ORDER:
            scan.copy1(d).start()
        scan.in1[p] = scan.out1[p]

    def send_group(scan, backward):
        for d in range(1, CHIPS):
            scan.copy1(d, True).wait_recv()
        total = jnp.zeros((SLICE, DH), F32)
        tail = jnp.zeros((8, DH), F32) if backward else jnp.ones((8, DH), F32)
        for s in range(CHIPS):
            at = CHIPS - 1 - s if backward else s
            total = fwd.in1[at, SLICE : SLICE + 1, :] * total + scan.in1[at, 0:SLICE, :]
            if backward:
                tail = tail + scan.in1[s, SLICE : SLICE + 8, :]
            else:
                tail = tail * scan.in1[s, SLICE : SLICE + 8, :]
        scan.out2[0:SLICE, :] = total
        scan.out2[SLICE : SLICE + 8, :] = tail
        for d in RING_ORDER:
            scan.copy2(d).start()
        scan.in2[g] = scan.out2[...]

    def send_back(scan, backward):
        for d in range(1, GROUPS):
            scan.copy2(d, True).wait_recv()
        state = jnp.zeros((SLICE, DH), F32)
        for s in range(GROUPS):
            at = GROUPS - 1 - s if backward else s
            later = fwd.in2[at, SLICE : SLICE + 1, :] * state + scan.in2[at, 0:SLICE, :]
            state = jnp.where(at > g if backward else at < g, later, state)
        for s in range(CHIPS):
            at = CHIPS - 1 - s if backward else s
            scan.out3[at] = state
            state = fwd.in1[at, SLICE : SLICE + 1, :] * state + scan.in1[at, 0:SLICE, :]
        for d in GROUP_ORDER:
            scan.copy3(d).start()
        scan.in3[p] = scan.out3[p]

    def receive(scan, backward, store):
        for d in range(1, CHIPS):
            scan.copy3(d, True).wait_recv()
        for j in range(2):
            half = CHIPS // 2
            entering = scan.in3[j * half : (j + 1) * half].reshape(DH, DH)
            theirs = scan.in0[j * DH : (j + 1) * DH, :]
            ours = own_st[j]
            d_ours, d_theirs = dec[mine + j], fwd.in0[2 * DH + j : 2 * DH + j + 1, :]
            past_ours = d_ours * entering + ours
            past_theirs = d_theirs * entering + theirs
            far = jnp.logical_not(first) if not backward else first
            store[mine + j] = jnp.where(far, past_theirs, entering)
            scan.out4[j] = jnp.where(far, entering, past_ours)
        scan.copy4().start()

    def intra_forward(h):
        for rb in range(NRB):
            rows = slice(rb * ROWB, (rb + 1) * ROWB)
            wide = (rb + 1) * ROWB
            raw = mm(q_ref[rows, lanes(h)], k_ref[0:wide, lanes(h)], 1, 1)
            col = rise[h, rows, :]
            for cb in range(rb + 1):
                cols = slice(cb * ROWB, (cb + 1) * ROWB)
                diff = col - crow[h, :, cols]
                if cb == rb:
                    i = lax.broadcasted_iota(jnp.int32, (ROWB, ROWB), 0)
                    j = lax.broadcasted_iota(jnp.int32, (ROWB, ROWB), 1)
                    diff = jnp.where(i >= j, diff, -jnp.inf)
                weight = jnp.exp(diff)
                w_st[h, rows, cols] = weight
                p_st[h, rows, cols] = (raw[:, cols] * weight).astype(BF16)
            a_st[rows, lanes(h)] = mm(p_st[h, rows, 0:wide], v_ref[0:wide, lanes(h)], 1, 0)

    def scale_upstream(h):
        su_st[:, lanes(h)] = u_ref[:, lanes(h)].astype(F32) * gain_ref[:, lanes(h)]

    def outer(h):
        hi, lo = split(s_st[h])
        for rb in range(NRB):
            rows = slice(rb * ROWB, (rb + 1) * ROWB)
            qq = q_ref[rows, lanes(h)]
            a_st[rows, lanes(h)] += jnp.exp(rise[h, rows, :]) * (mm(qq, hi, 1, 0) + mm(qq, lo, 1, 0))

    def intra_backward(h):
        hi, lo = split(s_st[h])
        for rb in range(NRB):
            rows = slice(rb * ROWB, (rb + 1) * ROWB)
            wide = (rb + 1) * ROWB
            dd = da_st[rows, lanes(h)]
            raw = mm(dd, v_ref[0:wide, lanes(h)], 1, 1)
            for cb in range(rb + 1):
                cols = slice(cb * ROWB, (cb + 1) * ROWB)
                g_st[rows, cols] = (raw[:, cols] * w_st[h, rows, cols]).astype(BF16)
            inner = mm(g_st[rows, 0:wide], k_ref[0:wide, lanes(h)], 1, 0)
            cross = mm(dd, hi, 1, 1) + mm(dd, lo, 1, 1)
            gq_ref[rows, lanes(h)] = (inner + jnp.exp(rise[h, rows, :]) * cross).astype(BF16)
        for cb in range(NRB):
            cols = slice(cb * ROWB, (cb + 1) * ROWB)
            below = slice(cb * ROWB, BLK)
            gk_st[cols, lanes(h)] = mm(g_st[below, cols], q_ref[below, lanes(h)], 0, 0)
            gv_st[cols, lanes(h)] = mm(p_st[h, below, cols], da_st[below, lanes(h)], 0, 0)

    def finish(h):
        hi, lo = split(r_st[h])
        for rb in range(NRB):
            rows = slice(rb * ROWB, (rb + 1) * ROWB)
            vv, kk, down = v_ref[rows, lanes(h)], k_ref[rows, lanes(h)], fall[h, rows, :]
            gk_ref[rows, lanes(h)] = (
                gk_st[rows, lanes(h)] + down * (mm(vv, hi, 1, 1) + mm(vv, lo, 1, 1))
            ).astype(BF16)
            gv_ref[rows, lanes(h)] = (
                gv_st[rows, lanes(h)] + down * (mm(kk, hi, 1, 0) + mm(kk, lo, 1, 0))
            ).astype(BF16)

    send_chip(fwd, False)
    intra_forward(0)
    intra_forward(1)
    send_group(fwd, False)
    intra_forward(2)
    intra_forward(3)
    send_back(fwd, False)
    for h in range(HEADS):
        scale_upstream(h)
    receive(fwd, False, s_st)
    for j in range(2):
        outer(mine + j)
    fwd.copy4().wait()
    for j in range(2):
        s_st[other + j] = fwd.in4[j]
        outer(other + j)

    for rb in range(NRB):
        rows = slice(rb * ROWB, (rb + 1) * ROWB)
        squares = jnp.zeros((ROWB, DH), F32)
        crosses = jnp.zeros((ROWB, DH), F32)
        for h in range(HEADS):
            act = a_st[rows, lanes(h)]
            squares = squares + act * act
            crosses = crosses + act * su_st[rows, lanes(h)]
        zout[rb : rb + 1, :] = jnp.sum(squares.T, axis=0, keepdims=True)
        zout[NRB + rb : NRB + rb + 1, :] = jnp.sum(crosses.T, axis=0, keepdims=True)
    for d in TP_ORDER:
        tp_copy(d).start()
    zin[tp] = zout[...]
    for d in range(1, TP):
        tp_copy(d, True).wait_recv()
    sums = zin[0]
    for s in range(1, TP):
        sums = sums + zin[s]
    inv_rms = lax.rsqrt(sums[0:NRB, :] / FEAT + 1e-06)
    pull = inv_rms * inv_rms * inv_rms * (sums[NRB : 2 * NRB, :] / FEAT)
    gain_terms = [jnp.zeros((1, DH), F32)] * HEADS
    for rb in range(NRB):
        rows = slice(rb * ROWB, (rb + 1) * ROWB)
        scale = bcast_col(inv_rms[rb : rb + 1, :])
        back = bcast_col(pull[rb : rb + 1, :])
        for h in range(HEADS):
            act = a_st[rows, lanes(h)]
            normed = act * scale
            out_ref[rows, lanes(h)] = (normed * gain_ref[:, lanes(h)]).astype(BF16)
            da_st[rows, lanes(h)] = (scale * su_st[rows, lanes(h)] - act * back).astype(BF16)
            gain_terms[h] = gain_terms[h] + jnp.sum(
                normed * u_ref[rows, lanes(h)].astype(F32), axis=0, keepdims=True
            )
    for h in range(HEADS):
        bwd.out0[2 * DH + h : 2 * DH + h + 1, :] = gain_terms[h]
    bwd.out0[2 * DH + 4 : 2 * DH + 8, :] = jnp.zeros((4, DH), F32)
    for j in range(2):
        bwd.out0[j * DH : (j + 1) * DH, :] = moment(other + j)
    bwd.copy0().start()
    for j in range(2):
        own_st[j] = moment(mine + j)
    send_chip(bwd, True)
    intra_backward(0)
    intra_backward(1)
    send_group(bwd, True)
    intra_backward(2)
    intra_backward(3)
    send_back(bwd, True)
    gain_sum = bwd.in2[0, SLICE : SLICE + 8, :]
    for s in range(1, GROUPS):
        gain_sum = gain_sum + bwd.in2[s, SLICE : SLICE + 8, :]
    for h in range(HEADS):
        gg_ref[:, lanes(h)] = gain_sum[h : h + 1, :]
    receive(bwd, True, r_st)
    for j in range(2):
        finish(mine + j)
    bwd.copy4().wait()
    for j in range(2):
        r_st[other + j] = bwd.in4[j]
        finish(other + j)

    for scan in (fwd, bwd):
        for d in range(1, CHIPS):
            scan.copy1(d).wait_send()
            scan.copy3(d).wait_send()
        for d in range(1, GROUPS):
            scan.copy2(d).wait_send()
    for d in range(1, TP):
        tp_copy(d).wait_send()


def scan_scratch():
    dma = pltpu.SemaphoreType.DMA
    wide = SLICE + 8
    return [
        pltpu.VMEM((2 * DH + 8, DH), F32),
        pltpu.VMEM((2 * DH + 8, DH), F32),
        pltpu.VMEM((CHIPS, wide, DH), F32),
        pltpu.VMEM((CHIPS, wide, DH), F32),
        pltpu.VMEM((wide, DH), F32),
        pltpu.VMEM((GROUPS, wide, DH), F32),
        pltpu.VMEM((CHIPS, SLICE, DH), F32),
        pltpu.VMEM((CHIPS, SLICE, DH), F32),
        pltpu.VMEM((2, DH, DH), F32),
        pltpu.VMEM((2, DH, DH), F32),
        dma((1,)), dma((1,)), dma((CHIPS,)), dma((CHIPS,)), dma((GROUPS,)),
        dma((GROUPS,)), dma((CHIPS,)), dma((CHIPS,)), dma((1,)), dma((1,)),
    ]


def body(queries, keys, values, log_decay, gain, upstream):
    vmem = pl.BlockSpec(memory_space=pltpu.VMEM)
    big = jax.ShapeDtypeStruct((BLK, HEADS * DH), BF16)
    dma = pltpu.SemaphoreType.DMA
    scratch = [
        pltpu.VMEM((HEADS, 1, BLK), F32),
        pltpu.VMEM((HEADS, BLK, DH), F32),
        pltpu.VMEM((HEADS, BLK, DH), F32),
        pltpu.VMEM((HEADS, 1, DH), F32),
        pltpu.VMEM((HEADS, BLK, BLK), F32),
        pltpu.VMEM((HEADS, BLK, BLK), BF16),
        pltpu.VMEM((BLK, BLK), BF16),
        pltpu.VMEM((BLK, HEADS * DH), F32),
        pltpu.VMEM((BLK, HEADS * DH), F32),
        pltpu.VMEM((BLK, HEADS * DH), BF16),
        pltpu.VMEM((BLK, HEADS * DH), F32),
        pltpu.VMEM((BLK, HEADS * DH), F32),
        pltpu.VMEM((2, DH, DH), F32),
        pltpu.VMEM((HEADS, DH, DH), F32),
        pltpu.VMEM((HEADS, DH, DH), F32),
        pltpu.VMEM((8, DH), F32),
        pltpu.VMEM((8, DH), F32),
        pltpu.VMEM((TP, 8, DH), F32),
        dma((TP,)),
        dma((TP,)),
    ]
    attn, gq, gk, gv, gg = pl.pallas_call(
        kernel,
        out_shape=(big, big, big, big, jax.ShapeDtypeStruct((1, HEADS * DH), F32)),
        in_specs=[vmem] * 6,
        out_specs=(vmem,) * 5,
        scratch_shapes=scratch + scan_scratch() + scan_scratch(),
        compiler_params=pltpu.CompilerParams(
            collective_id=0, has_side_effects=True, vmem_limit_bytes=40 * 2**20
        ),
        name="attention",
    )(queries, keys, values, log_decay.T, gain.reshape(1, HEADS * DH), upstream)
    return attn, gq, gk, gv, gg.reshape(HEADS * DH)


def solution(mesh):
    placed = (P("ctx", "tp"),) * 4 + (P("tp"), P("ctx", "tp"))
    return jax.shard_map(
        body,
        mesh=mesh,
        in_specs=placed,
        out_specs=(P("ctx", "tp"),) * 4 + (P("tp"),),
        check_vma=False,
    )
```

```python
import functools

import jax
import jax.numpy as jnp
from jax import lax
from jax.experimental import pallas as pl
from jax.experimental.pallas import tpu as pltpu
from jax.sharding import PartitionSpec as P

MESH = pl.DeviceIdType.MESH
FEAT = 4096
BLK = 512
DH = 128
HEADS = 4
ROWB = 128
NRB = BLK // ROWB
CHIPS = 8
GROUPS = 4
TP = 8
SLICE = 2 * DH // CHIPS
F32 = jnp.float32
BF16 = jnp.bfloat16


def mm(a, b, ca, cb):
    return lax.dot_general(a, b, (((ca,), (cb,)), ((), ())), preferred_element_type=F32)


def split(x):
    hi = x.astype(BF16)
    return hi, (x - hi.astype(F32)).astype(BF16)


def bcast_col(row):
    return jnp.broadcast_to(row, (ROWB, row.shape[1])).T


class Scan:
    def __init__(self, refs, place):
        (
            self.out0, self.in0, self.out1, self.in1, self.out2, self.in2, self.out3, self.in3, self.out4, self.in4,
            self.s0, self.r0, self.s1, self.r1, self.s2, self.r2, self.s3, self.r3, self.s4, self.r4,
        ) = refs
        self.core, self.p, self.g, self.tp = place

    def device(self, g, p, core):
        return ((g * CHIPS + p) * 2 + core, self.tp)

    def core_copy(self, src, dst, send, recv):
        return pltpu.make_async_remote_copy(
            src_ref=src, dst_ref=dst, send_sem=send.at[0], recv_sem=recv.at[0],
            device_id=self.device(self.g, self.p, 1 - self.core), device_id_type=MESH,
        )

    def copy0(self):
        return self.core_copy(self.out0, self.in0, self.s0, self.r0)

    def copy4(self):
        return self.core_copy(self.out4, self.in4, self.s4, self.r4)

    def group_copy(self, d, src, dst, send, recv, arriving):
        peer = (self.p + d) % CHIPS
        slot = peer if arriving else self.p
        return pltpu.make_async_remote_copy(
            src_ref=src.at[peer], dst_ref=dst.at[slot], send_sem=send.at[d], recv_sem=recv.at[slot],
            device_id=self.device(self.g, peer, self.core), device_id_type=MESH,
        )

    def copy1(self, d, arriving=False):
        return self.group_copy(d, self.out1, self.in1, self.s1, self.r1, arriving)

    def copy3(self, d, arriving=False):
        return self.group_copy(d, self.out3, self.in3, self.s3, self.r3, arriving)

    def copy2(self, d, arriving=False):
        peer = (self.g + d) % GROUPS
        slot = peer if arriving else self.g
        return pltpu.make_async_remote_copy(
            src_ref=self.out2, dst_ref=self.in2.at[slot], send_sem=self.s2.at[d], recv_sem=self.r2.at[slot],
            device_id=self.device(peer, self.p, self.core), device_id_type=MESH,
        )


GROUP_ORDER = (6, 2, 4, 5, 3, 7, 1)
RING_ORDER = (2, 1, 3)
TP_ORDER = (4, 3, 5, 2, 6, 1, 7)


def finish_head(columns, state, fall, v_ref, k_ref, gk_st, gv_st, gk_ref, gv_ref):
    hi, lo = split(state)
    for rb in range(NRB):
        rows = slice(rb * ROWB, (rb + 1) * ROWB)
        vv, kk, down = v_ref[rows, columns], k_ref[rows, columns], fall[rows, :]
        gk_ref[rows, columns] = (
            gk_st[rows, columns] + down * (mm(vv, hi, 1, 1) + mm(vv, lo, 1, 1))
        ).astype(BF16)
        gv_ref[rows, columns] = (
            gv_st[rows, columns] + down * (mm(kk, hi, 1, 0) + mm(kk, lo, 1, 0))
        ).astype(BF16)


def tail_kernel(
    out_in, gq_in, gk_in, gv_in, gg_in, gk_st, gv_st, r_st, fall, k_ref, v_ref,
    out_hbm, gq_hbm, gk_hbm, gv_hbm, gg_hbm, gk_ref, gv_ref, sem,
):
    core = lax.axis_index("ctx") % 2

    def half_store(src, dst, which, at):
        columns = pl.ds(pl.multiple_of(which * 2 * DH, 2 * DH), 2 * DH)
        return pltpu.make_async_copy(src.at[:, columns], dst.at[:, columns], sem.at[at])

    stores = [
        pltpu.make_async_copy(out_in, out_hbm, sem.at[0]),
        pltpu.make_async_copy(gq_in, gq_hbm, sem.at[1]),
        pltpu.make_async_copy(gg_in, gg_hbm, sem.at[2]),
        half_store(gk_in, gk_hbm, core, 3),
        half_store(gv_in, gv_hbm, core, 4),
    ]
    for store in stores:
        store.start()
    for j in range(2):
        h = 2 * (1 - core) + j
        columns = pl.ds(pl.multiple_of(h * DH, DH), DH)
        finish_head(columns, r_st[h], fall.at[h], v_ref, k_ref, gk_st, gv_st, gk_ref, gv_ref)
    last = [half_store(gk_ref, gk_hbm, 1 - core, 5), half_store(gv_ref, gv_hbm, 1 - core, 6)]
    for store in last:
        store.start()
    for store in stores + last:
        store.wait()


def kernel(*refs):
    (q_hbm, k_hbm, v_hbm, log_hbm, gain_hbm, u_hbm) = refs[:6]
    (out_ref, gq_ref, gk_ref, gv_ref, gg_ref, gk_st, gv_st, r_st, fall, k_ref, v_ref) = refs[6:17]
    (
        q_ref, log_ref, gain_ref, u_ref, crow, rise, dec, w_st, p_st, g_st, a_st, su_st, da_st, own_st, s_st,
        zout, zin, zs, zr, load_sem,
    ) = refs[17:37]
    ctx = lax.axis_index("ctx")
    tp = lax.axis_index("tp")
    core = ctx % 2
    chip = ctx // 2
    p = chip % CHIPS
    g = chip // CHIPS
    place = (core, p, g, tp)
    fwd = Scan(refs[37:57], place)
    bwd = Scan(refs[57:77], place)
    first = core == 0

    def tp_copy(d, arriving=False):
        peer = (tp + d) % TP
        slot = peer if arriving else tp
        return pltpu.make_async_remote_copy(
            src_ref=zout, dst_ref=zin.at[slot], send_sem=zs.at[d], recv_sem=zr.at[slot],
            device_id=(ctx, peer), device_id_type=MESH,
        )

    def half_load(src, dst, which, at):
        columns = pl.ds(pl.multiple_of(which * 2 * DH, 2 * DH), 2 * DH)
        return pltpu.make_async_copy(src.at[:, columns], dst.at[:, columns], load_sem.at[at])

    log_load = pltpu.make_async_copy(log_hbm, log_ref, load_sem.at[0])
    far_loads = [half_load(k_hbm, k_ref, 1 - core, 1), half_load(v_hbm, v_ref, 1 - core, 2)]
    near_loads = [half_load(k_hbm, k_ref, core, 3), half_load(v_hbm, v_ref, core, 4)]
    late_loads = [
        pltpu.make_async_copy(q_hbm, q_ref, load_sem.at[5]),
        pltpu.make_async_copy(u_hbm, u_ref, load_sem.at[6]),
        pltpu.make_async_copy(gain_hbm, gain_ref, load_sem.at[7]),
    ]
    for load in [log_load] + far_loads + near_loads + late_loads:
        load.start()

    barrier = pltpu.get_barrier_semaphore()
    partners = [fwd.device(g, p, 1 - core)]
    partners += [fwd.device(g, (p + d) % CHIPS, core) for d in range(1, CHIPS)]
    partners += [fwd.device((g + d) % GROUPS, p, core) for d in range(1, GROUPS)]
    partners += [(ctx, (tp + d) % TP) for d in range(1, TP)]
    for partner in partners:
        pl.semaphore_signal(barrier, inc=1, device_id=partner, device_id_type=MESH)

    log_load.wait()
    cum = log_ref[...]
    lane = lax.broadcasted_iota(jnp.int32, cum.shape, 1)
    step = 1
    while step < BLK:
        cum = cum + jnp.where(lane >= step, pltpu.roll(cum, step, axis=1), 0.0)
        step *= 2
    for h in range(HEADS):
        row = cum[h : h + 1, :]
        crow[h] = row
        last = jnp.broadcast_to(row[:, BLK - 1 : BLK], (1, DH))
        dec[h] = jnp.exp(last)
        for rb in range(NRB):
            rows = slice(rb * ROWB, (rb + 1) * ROWB)
            col = bcast_col(row[:, rows])
            rise[h, rows, :] = col
            fall[h, rows, :] = jnp.exp(last - col)

    def lanes(h):
        if isinstance(h, int):
            return slice(h * DH, (h + 1) * DH)
        return pl.ds(pl.multiple_of(h * DH, DH), DH)

    def keyed_state(h):
        total = None
        for rb in range(NRB):
            rows = slice(rb * ROWB, (rb + 1) * ROWB)
            hi, lo = split(k_ref[rows, lanes(h)].astype(F32) * fall[h, rows, :])
            vv = v_ref[rows, lanes(h)]
            term = mm(hi, vv, 0, 0) + mm(lo, vv, 0, 0)
            total = term if total is None else total + term
        return total

    def moment(h):
        total = None
        for rb in range(NRB):
            rows = slice(rb * ROWB, (rb + 1) * ROWB)
            hi, lo = split(q_ref[rows, lanes(h)].astype(F32) * jnp.exp(rise[h, rows, :]))
            dd = da_st[rows, lanes(h)]
            term = mm(hi, dd, 0, 0) + mm(lo, dd, 0, 0)
            total = term if total is None else total + term
        return total

    mine = 2 * core
    other = 2 * (1 - core)
    for load in far_loads:
        load.wait()
    for j in range(2):
        fwd.out0[j * DH : (j + 1) * DH, :] = keyed_state(other + j)
        fwd.out0[2 * DH + j : 2 * DH + j + 1, :] = dec[other + j]
    fwd.out0[2 * DH + 2 : 2 * DH + 8, :] = jnp.zeros((6, DH), F32)
    pl.semaphore_wait(barrier, len(partners))
    fwd.copy0().start()
    for load in near_loads:
        load.wait()
    for j in range(2):
        own_st[j] = keyed_state(mine + j)

    def send_chip(scan, backward):
        scan.copy0().wait()
        for j in range(2):
            theirs = scan.in0[j * DH : (j + 1) * DH, :]
            ours = own_st[j]
            d_ours, d_theirs = dec[mine + j], fwd.in0[2 * DH + j : 2 * DH + j + 1, :]
            if backward:
                chip_state = jnp.where(first, d_ours * theirs + ours, d_theirs * ours + theirs)
                tail = scan.in0[2 * DH : 2 * DH + 8, :] + scan.out0[2 * DH : 2 * DH + 8, :]
            else:
                chip_state = jnp.where(first, d_theirs * ours + theirs, d_ours * theirs + ours)
                tail = jnp.broadcast_to(d_ours * d_theirs, (8, DH))
            for piece in range(CHIPS // 2):
                slot = j * (CHIPS // 2) + piece
                scan.out1[slot, 0:SLICE, :] = chip_state[piece * SLICE : (piece + 1) * SLICE, :]
                scan.out1[slot, SLICE : SLICE + 8, :] = tail
        for d in GROUP_ORDER:
            scan.copy1(d).start()
        scan.in1[p] = scan.out1[p]

    def send_group(scan, backward):
        for d in range(1, CHIPS):
            scan.copy1(d, True).wait_recv()
        total = jnp.zeros((SLICE, DH), F32)
        tail = jnp.zeros((8, DH), F32) if backward else jnp.ones((8, DH), F32)
        for s in range(CHIPS):
            at = CHIPS - 1 - s if backward else s
            total = fwd.in1[at, SLICE : SLICE + 1, :] * total + scan.in1[at, 0:SLICE, :]
            if backward:
                tail = tail + scan.in1[s, SLICE : SLICE + 8, :]
            else:
                tail = tail * scan.in1[s, SLICE : SLICE + 8, :]
        scan.out2[0:SLICE, :] = total
        scan.out2[SLICE : SLICE + 8, :] = tail
        for d in RING_ORDER:
            scan.copy2(d).start()
        scan.in2[g] = scan.out2[...]

    def send_back(scan, backward):
        for d in range(1, GROUPS):
            scan.copy2(d, True).wait_recv()
        state = jnp.zeros((SLICE, DH), F32)
        for s in range(GROUPS):
            at = GROUPS - 1 - s if backward else s
            later = fwd.in2[at, SLICE : SLICE + 1, :] * state + scan.in2[at, 0:SLICE, :]
            state = jnp.where(at > g if backward else at < g, later, state)
        for s in range(CHIPS):
            at = CHIPS - 1 - s if backward else s
            scan.out3[at] = state
            state = fwd.in1[at, SLICE : SLICE + 1, :] * state + scan.in1[at, 0:SLICE, :]
        for d in GROUP_ORDER:
            scan.copy3(d).start()
        scan.in3[p] = scan.out3[p]

    def receive(scan, backward, store):
        for d in range(1, CHIPS):
            scan.copy3(d, True).wait_recv()
        for j in range(2):
            half = CHIPS // 2
            entering = scan.in3[j * half : (j + 1) * half].reshape(DH, DH)
            theirs = scan.in0[j * DH : (j + 1) * DH, :]
            ours = own_st[j]
            d_ours, d_theirs = dec[mine + j], fwd.in0[2 * DH + j : 2 * DH + j + 1, :]
            past_ours = d_ours * entering + ours
            past_theirs = d_theirs * entering + theirs
            far = jnp.logical_not(first) if not backward else first
            store[mine + j] = jnp.where(far, past_theirs, entering)
            scan.out4[j] = jnp.where(far, entering, past_ours)
        scan.copy4().start()

    def intra_forward(h):
        for rb in range(NRB):
            rows = slice(rb * ROWB, (rb + 1) * ROWB)
            wide = (rb + 1) * ROWB
            raw = mm(q_ref[rows, lanes(h)], k_ref[0:wide, lanes(h)], 1, 1)
            col = rise[h, rows, :]
            for cb in range(rb + 1):
                cols = slice(cb * ROWB, (cb + 1) * ROWB)
                diff = col - crow[h, :, cols]
                if cb == rb:
                    i = lax.broadcasted_iota(jnp.int32, (ROWB, ROWB), 0)
                    j = lax.broadcasted_iota(jnp.int32, (ROWB, ROWB), 1)
                    diff = jnp.where(i >= j, diff, -jnp.inf)
                weight = jnp.exp(diff)
                w_st[h, rows, cols] = weight
                p_st[h, rows, cols] = (raw[:, cols] * weight).astype(BF16)
            a_st[rows, lanes(h)] = mm(p_st[h, rows, 0:wide], v_ref[0:wide, lanes(h)], 1, 0)

    def scale_upstream(h):
        su_st[:, lanes(h)] = u_ref[:, lanes(h)].astype(F32) * gain_ref[:, lanes(h)]

    def outer(h):
        hi, lo = split(s_st[h])
        for rb in range(NRB):
            rows = slice(rb * ROWB, (rb + 1) * ROWB)
            qq = q_ref[rows, lanes(h)]
            a_st[rows, lanes(h)] += jnp.exp(rise[h, rows, :]) * (mm(qq, hi, 1, 0) + mm(qq, lo, 1, 0))

    def intra_backward(h):
        hi, lo = split(s_st[h])
        for rb in range(NRB):
            rows = slice(rb * ROWB, (rb + 1) * ROWB)
            wide = (rb + 1) * ROWB
            dd = da_st[rows, lanes(h)]
            raw = mm(dd, v_ref[0:wide, lanes(h)], 1, 1)
            for cb in range(rb + 1):
                cols = slice(cb * ROWB, (cb + 1) * ROWB)
                g_st[rows, cols] = (raw[:, cols] * w_st[h, rows, cols]).astype(BF16)
            inner = mm(g_st[rows, 0:wide], k_ref[0:wide, lanes(h)], 1, 0)
            cross = mm(dd, hi, 1, 1) + mm(dd, lo, 1, 1)
            gq_ref[rows, lanes(h)] = (inner + jnp.exp(rise[h, rows, :]) * cross).astype(BF16)
        for cb in range(NRB):
            cols = slice(cb * ROWB, (cb + 1) * ROWB)
            below = slice(cb * ROWB, BLK)
            gk_st[cols, lanes(h)] = mm(g_st[below, cols], q_ref[below, lanes(h)], 0, 0)
            gv_st[cols, lanes(h)] = mm(p_st[h, below, cols], da_st[below, lanes(h)], 0, 0)

    def finish(h):
        finish_head(lanes(h), r_st[h], fall.at[h], v_ref, k_ref, gk_st, gv_st, gk_ref, gv_ref)

    send_chip(fwd, False)
    for load in late_loads:
        load.wait()
    intra_forward(0)
    intra_forward(1)
    send_group(fwd, False)
    intra_forward(2)
    intra_forward(3)
    send_back(fwd, False)
    for h in range(HEADS):
        scale_upstream(h)
    receive(fwd, False, s_st)
    for j in range(2):
        outer(mine + j)
    fwd.copy4().wait()
    for j in range(2):
        s_st[other + j] = fwd.in4[j]
        outer(other + j)

    for rb in range(NRB):
        rows = slice(rb * ROWB, (rb + 1) * ROWB)
        squares = jnp.zeros((ROWB, DH), F32)
        crosses = jnp.zeros((ROWB, DH), F32)
        for h in range(HEADS):
            act = a_st[rows, lanes(h)]
            squares = squares + act * act
            crosses = crosses + act * su_st[rows, lanes(h)]
        zout[rb : rb + 1, :] = jnp.sum(squares.T, axis=0, keepdims=True)
        zout[NRB + rb : NRB + rb + 1, :] = jnp.sum(crosses.T, axis=0, keepdims=True)
    for d in TP_ORDER:
        tp_copy(d).start()
    zin[tp] = zout[...]
    for d in range(1, TP):
        tp_copy(d, True).wait_recv()
    sums = zin[0]
    for s in range(1, TP):
        sums = sums + zin[s]
    inv_rms = lax.rsqrt(sums[0:NRB, :] / FEAT + 1e-06)
    pull = inv_rms * inv_rms * inv_rms * (sums[NRB : 2 * NRB, :] / FEAT)
    gain_terms = [jnp.zeros((1, DH), F32)] * HEADS
    for rb in range(NRB):
        rows = slice(rb * ROWB, (rb + 1) * ROWB)
        scale = bcast_col(inv_rms[rb : rb + 1, :])
        back = bcast_col(pull[rb : rb + 1, :])
        for h in range(HEADS):
            act = a_st[rows, lanes(h)]
            normed = act * scale
            out_ref[rows, lanes(h)] = (normed * gain_ref[:, lanes(h)]).astype(BF16)
            da_st[rows, lanes(h)] = (scale * su_st[rows, lanes(h)] - act * back).astype(BF16)
            gain_terms[h] = gain_terms[h] + jnp.sum(
                normed * u_ref[rows, lanes(h)].astype(F32), axis=0, keepdims=True
            )
    for h in range(HEADS):
        bwd.out0[2 * DH + h : 2 * DH + h + 1, :] = gain_terms[h]
    bwd.out0[2 * DH + 4 : 2 * DH + 8, :] = jnp.zeros((4, DH), F32)
    for j in range(2):
        bwd.out0[j * DH : (j + 1) * DH, :] = moment(other + j)
    bwd.copy0().start()
    for j in range(2):
        own_st[j] = moment(mine + j)
    send_chip(bwd, True)
    intra_backward(0)
    intra_backward(1)
    send_group(bwd, True)
    intra_backward(2)
    intra_backward(3)
    send_back(bwd, True)
    gain_sum = bwd.in2[0, SLICE : SLICE + 8, :]
    for s in range(1, GROUPS):
        gain_sum = gain_sum + bwd.in2[s, SLICE : SLICE + 8, :]
    for h in range(HEADS):
        gg_ref[:, lanes(h)] = gain_sum[h : h + 1, :]
    receive(bwd, True, r_st)
    for j in range(2):
        finish(mine + j)
    bwd.copy4().wait()
    for j in range(2):
        r_st[other + j] = bwd.in4[j]

    for scan in (fwd, bwd):
        for d in range(1, CHIPS):
            scan.copy1(d).wait_send()
            scan.copy3(d).wait_send()
        for d in range(1, GROUPS):
            scan.copy2(d).wait_send()
    for d in range(1, TP):
        tp_copy(d).wait_send()


def scan_scratch():
    dma = pltpu.SemaphoreType.DMA
    wide = SLICE + 8
    return [
        pltpu.VMEM((2 * DH + 8, DH), F32),
        pltpu.VMEM((2 * DH + 8, DH), F32),
        pltpu.VMEM((CHIPS, wide, DH), F32),
        pltpu.VMEM((CHIPS, wide, DH), F32),
        pltpu.VMEM((wide, DH), F32),
        pltpu.VMEM((GROUPS, wide, DH), F32),
        pltpu.VMEM((CHIPS, SLICE, DH), F32),
        pltpu.VMEM((CHIPS, SLICE, DH), F32),
        pltpu.VMEM((2, DH, DH), F32),
        pltpu.VMEM((2, DH, DH), F32),
        dma((1,)), dma((1,)), dma((CHIPS,)), dma((CHIPS,)), dma((GROUPS,)),
        dma((GROUPS,)), dma((CHIPS,)), dma((CHIPS,)), dma((1,)), dma((1,)),
    ]


def body(queries, keys, values, log_decay, gain, upstream):
    vmem = pl.BlockSpec(memory_space=pltpu.VMEM)
    big = jax.ShapeDtypeStruct((BLK, HEADS * DH), BF16)
    dma = pltpu.SemaphoreType.DMA
    row = jax.ShapeDtypeStruct((1, HEADS * DH), F32)
    full = jax.ShapeDtypeStruct((BLK, HEADS * DH), F32)
    states = jax.ShapeDtypeStruct((HEADS, DH, DH), F32)
    columns = jax.ShapeDtypeStruct((HEADS, BLK, DH), F32)
    scratch = [
        pltpu.VMEM((BLK, HEADS * DH), BF16),
        pltpu.VMEM((HEADS, BLK), F32),
        pltpu.VMEM((1, HEADS * DH), F32),
        pltpu.VMEM((BLK, HEADS * DH), BF16),
        pltpu.VMEM((HEADS, 1, BLK), F32),
        pltpu.VMEM((HEADS, BLK, DH), F32),
        pltpu.VMEM((HEADS, 1, DH), F32),
        pltpu.VMEM((HEADS, BLK, BLK), F32),
        pltpu.VMEM((HEADS, BLK, BLK), BF16),
        pltpu.VMEM((BLK, BLK), BF16),
        pltpu.VMEM((BLK, HEADS * DH), F32),
        pltpu.VMEM((BLK, HEADS * DH), F32),
        pltpu.VMEM((BLK, HEADS * DH), BF16),
        pltpu.VMEM((2, DH, DH), F32),
        pltpu.VMEM((HEADS, DH, DH), F32),
        pltpu.VMEM((8, DH), F32),
        pltpu.VMEM((TP, 8, DH), F32),
        dma((TP,)),
        dma((TP,)),
        dma((8,)),
    ]
    hbm = pl.BlockSpec(memory_space=pltpu.HBM)
    held = pl.pallas_call(
        kernel,
        out_shape=(big, big, big, big, row, full, full, states, columns, big, big),
        in_specs=[hbm] * 6,
        out_specs=(vmem,) * 11,
        scratch_shapes=scratch + scan_scratch() + scan_scratch(),
        compiler_params=pltpu.CompilerParams(
            collective_id=0, has_side_effects=True, vmem_limit_bytes=40 * 2**20
        ),
        name="attention",
    )(*(pltpu.with_memory_space_constraint(x, pltpu.HBM) for x in (queries, keys, values, log_decay.T, gain.reshape(1, HEADS * DH), upstream)))
    attn, gq, gk, gv, gg = pl.pallas_call(
        tail_kernel,
        out_shape=(big, big, big, big, row),
        in_specs=[vmem] * 11,
        out_specs=(hbm,) * 5,
        scratch_shapes=[
            pltpu.VMEM((BLK, HEADS * DH), BF16),
            pltpu.VMEM((BLK, HEADS * DH), BF16),
            dma((7,)),
        ],
        compiler_params=pltpu.CompilerParams(vmem_limit_bytes=24 * 2**20),
        name="finish",
    )(*held)
    return attn, gq, gk, gv, gg.reshape(HEADS * DH)


def solution(mesh):
    placed = (P("ctx", "tp"),) * 4 + (P("tp"), P("ctx", "tp"))
    return jax.shard_map(
        body,
        mesh=mesh,
        in_specs=placed,
        out_specs=(P("ctx", "tp"),) * 4 + (P("tp"),),
        check_vma=False,
    )
```
